512 devices in a mesh: leaf: 64 (over z_lo, x, y), head: 8 (over z_hi, core).
Axes of the slice: x: 4, y: 8, z: 8 (z_hi: 4, z_lo: 2; z = z_hi * 2 + z_lo), core: 2. Of those that a mesh axis runs over, the one named last changes fastest.
Arguments:
- queries: bfloat16 [8192, 64, 576], P('leaf', 'head'), may hold values from -40 to 40
- leaf_latent: bfloat16 [8192, 576], P('leaf'), may hold values from -4 to 4
- node_latent: bfloat16 [64, 96, 576], P('leaf', 'head'), may hold values from -4 to 4
- grad_out: bfloat16 [8192, 64, 512], P('leaf', 'head'), may hold values from -6 to 6
- leaf_nodes: int32 [128, 3], P('leaf'), may hold values from 0 to 63, as said below
- leaf_lengths: int32 [128], P('leaf'), may hold values from 1 to 64, 5120 in all
Outputs:
- attention: bfloat16 [8192, 64, 512], P('leaf', 'head')
- node_grad: bfloat16 [64, 96, 576], P('leaf', 'head')
- leaf_grad: bfloat16 [8192, 576], P('leaf')
The draws below stay inside these ranges and needn't reach their ends.
Inputs may be any that keep to these rules, and one draw needn't show every extreme that they name: `leaf_nodes`: each row lists three different nodes: a root, one of its children and one of that child's children. Every node has one level and one parent; which nodes are used and how often varies.
All inputs are finite; a program needn't handle non-finite values. No bound on the sum of `leaf_lengths` on one device may be relied on, other than what follows from the above.
Results may differ from the reference program's by a relative error of at most 0.0095.
Values may be sent and summed in bfloat16 or wider, within the bound.
A program may use at most 64 MiB of HBM per device.

```python
import math
import jax
import jax.numpy as jnp
import numpy as np
from jax import lax

LAT = 512
LEAF_ROWS = 64
NODE_ROWS = 96
LATW = 576
HEADS = 64
LEAVES = 128
ROWS = 8192
NODES = 64
KEYS = 352


def leaf_pair(key):
    base = jax.random.fold_in(key, 4242)
    key_lat, key_query = jax.random.split(base, 2)
    latent = jnp.clip(jax.random.normal(key_lat, (ROWS, LATW), jnp.float32), -4.0, 4.0).astype(jnp.bfloat16)
    query = jnp.clip(jax.random.normal(key_query, (ROWS, HEADS, LATW), jnp.float32), -6.0, 6.0)
    return (query.astype(jnp.bfloat16), latent)


def draw_queries(key, part):
    return leaf_pair(key)[0]


def draw_leaf_latent(key, part):
    return leaf_pair(key)[1]


def draw_leaf_nodes(key, part):
    base = jax.random.fold_in(key, 31)
    key_order, key_first, key_second = jax.random.split(base, 3)
    roots = max(NODES // 16, 1)
    middle = NODES * 3 // 16
    deepest = NODES - roots - middle
    order = jax.random.permutation(key_order, NODES)
    picked = jnp.minimum(jax.random.randint(key_first, (LEAVES,), 0, deepest), jax.random.randint(key_second, (LEAVES,), 0, deepest))
    middle_of = picked % middle
    root_of = middle_of % roots
    return jnp.stack([order[root_of], order[roots + middle_of], order[roots + middle + picked]], axis=1).astype(jnp.int32)


def shard_levels(key, shape, cuts, low, largest):
    def one(dim, blocks):
        heights = jax.random.uniform(jax.random.fold_in(jax.random.fold_in(key, 6), dim), (blocks,), jnp.float32, low / len(cuts), largest / len(cuts))
        return jnp.repeat(jnp.exp(heights), shape[dim] // blocks).reshape((-1,) + (1,) * (len(shape) - dim - 1))

    gain = one(*cuts[0])
    for cut in cuts[1:]:
        gain = gain * one(*cut)
    return gain


def profile(number_of, total, bound, lean):
    portions = [(1 << 20) // math.isqrt(standing ** lean) + 1 for standing in range(2, number_of + 1)]
    rest, given = total - bound - (number_of - 1), [1] * (number_of - 1)
    while rest > 0:
        movable = [i for i in range(number_of - 1) if given[i] < bound]
        mass, left = sum([portions[i] for i in movable]), rest
        for i in movable:
            addition = min(bound - given[i], max(1, left * portions[i] // mass), rest)
            given[i] = given[i] + addition
            rest = rest - addition
    return np.array([bound] + given)


def uneven(own_key, number_of, total, most, lean):
    if number_of == 2:
        one = jax.random.randint(own_key, (), max(1, total - most), min(most, total - 1) + 1)
        return jnp.stack([one, total - one])
    lengths = jnp.asarray(profile(number_of, total, most, lean), jnp.int32)
    pairs = (number_of - 1) // 2
    donor, sink = lengths[1:1 + 2 * pairs:2], lengths[2:2 + 2 * pairs:2]
    margin = jnp.minimum(donor - 1, most - sink)
    moved = jax.random.randint(jax.random.fold_in(own_key, 1), (pairs,), 0, 1 << 20) % (margin + 1)
    lengths = lengths.at[1:1 + 2 * pairs:2].set(donor - moved).at[2:2 + 2 * pairs:2].set(sink + moved)
    return lengths[jax.random.permutation(jax.random.fold_in(own_key, 2), number_of)]


def scatter_about(stream_key, shape, spread, bound, shards=(), kind=jnp.bfloat16):
    gain = shard_levels(stream_key, shape, shards, -0.22, 0.18) if shards else 1.0
    result = jax.random.normal(stream_key, shape, jnp.float32) * spread * gain
    return jnp.minimum(jnp.maximum(result, -bound), bound).astype(kind)


def setup_inputs(seed: int = 0) -> dict:
    splits = jax.random.split(jax.random.key(seed), 7)
    queries = draw_queries(jax.random.fold_in(splits[6], 71), 0)
    leaf_latent = draw_leaf_latent(jax.random.fold_in(splits[6], 71), 0)
    node_latent = scatter_about(splits[2], (NODES, NODE_ROWS, LATW), 1.0, 4.0, ((0, 64), (1, 8)))
    grad_out = scatter_about(splits[3], (ROWS, HEADS, LAT), 1.0, 6.0, ((0, 64), (1, 8)))
    leaf_nodes = draw_leaf_nodes(jax.random.fold_in(splits[6], 71), 0)
    leaf_lengths = uneven(splits[5], LEAVES, LEAVES * LEAF_ROWS * 5 // 8, LEAF_ROWS, 2).astype(jnp.int32)
    return dict(queries=queries, leaf_latent=leaf_latent, node_latent=node_latent, grad_out=grad_out, leaf_nodes=leaf_nodes, leaf_lengths=leaf_lengths)


score_scale = 192.0 ** -0.5


def reference(queries, leaf_latent, node_latent, grad_out, leaf_nodes, leaf_lengths):
    q_all = queries.reshape(LEAVES, LEAF_ROWS, HEADS, LATW)
    lat_all = leaf_latent.reshape(LEAVES, LEAF_ROWS, LATW)
    dout_all = grad_out.reshape(LEAVES, LEAF_ROWS, HEADS, LAT)
    row_index = jnp.arange(LEAF_ROWS, dtype=jnp.int32)
    key_index = jnp.arange(KEYS, dtype=jnp.int32)
    visible = (key_index[None, :] < 3 * NODE_ROWS) | ((key_index[None, :] - 3 * NODE_ROWS) <= row_index[:, None])

    def one_leaf(accum, items):
        query, own, dout, ids, length = items
        keys = jnp.concatenate([node_latent[ids].reshape(3 * NODE_ROWS, LATW), own], axis=0)
        live = (row_index < length).astype(jnp.float32)
        keys_f = keys.astype(jnp.float32)
        values_f = keys_f[:, :LAT]
        query_f = query.astype(jnp.float32)
        scores = jnp.einsum('rhc,kc->rhk', query_f, keys_f) * score_scale
        scores = jnp.where(visible[:, None, :], scores, -jnp.inf)
        top = jnp.max(scores, axis=-1, keepdims=True)
        expo = jnp.exp(scores - top)
        probs = expo / jnp.sum(expo, axis=-1, keepdims=True)
        probs_b = probs.astype(jnp.bfloat16).astype(jnp.float32)
        outputs = jnp.einsum('rhk,kc->rhc', probs_b, values_f)
        attn = (outputs * live[:, None, None]).astype(jnp.bfloat16)
        masked = (dout.astype(jnp.float32) * live[:, None, None]).astype(jnp.bfloat16).astype(jnp.float32)
        dprobs = jnp.einsum('rhc,kc->rhk', masked, values_f)
        delta = jnp.sum(masked * outputs, axis=-1)
        dscores = (score_scale * probs * (dprobs - delta[..., None])).astype(jnp.bfloat16).astype(jnp.float32)
        grad_keys = jnp.einsum('rhk,rhc->kc', dscores, query_f)
        grad_values = jnp.einsum('rhk,rhc->kc', probs_b, masked)
        grad_keys = jnp.concatenate([grad_keys[:, :LAT] + grad_values, grad_keys[:, LAT:]], axis=1)
        accum = accum.at[ids].add(grad_keys[:3 * NODE_ROWS].reshape(3, NODE_ROWS, LATW))
        return accum, (attn, grad_keys[3 * NODE_ROWS:].astype(jnp.bfloat16))

    start = jnp.zeros((NODES, NODE_ROWS, LATW), jnp.float32)
    accum, (attn, own_grad) = lax.scan(one_leaf, start, (q_all, lat_all, dout_all, leaf_nodes.astype(jnp.int32), leaf_lengths.astype(jnp.int32)))
    return attn.reshape(ROWS, HEADS, LAT), accum.astype(jnp.bfloat16), own_grad.reshape(ROWS, LATW)
```

```python
import functools

import jax
import jax.numpy as jnp
from jax import lax
from jax.experimental import pallas as pl
from jax.experimental.pallas import tpu as pltpu
from jax.sharding import PartitionSpec as P

MESH = pl.DeviceIdType.MESH
ZLO, XS, YS, ZHI = 2, 4, 8, 4
LAT = 512
LATW = 576
SLICE = 12
UNIT = 32
score_scale = 192.0 ** (-0.5)
F32 = jnp.float32
BF16 = jnp.bfloat16


def place():
    leaf, head = lax.axis_index("leaf"), lax.axis_index("head")
    return leaf // (XS * YS), (leaf // YS) % XS, leaf % YS, head // 2, head % 2


def device(zlo, x, y, zhi, core):
    return ((zlo * XS + x) * YS + y, zhi * 2 + core)


def pack(rows, ref, at):
    for block in range(4):
        part, below = block // 2, block % 2
        ref[part, at + below * SLICE : at + (below + 1) * SLICE, :] = rows[
            :, block * 128 : (block + 1) * 128
        ]
    ref[1, at + 24 : at + 30, :] = jnp.concatenate(
        [rows[0:6, LAT:LATW], rows[6:12, LAT:LATW]], axis=1
    )


def unpack(part, value, ref, at):
    for below in range(2):
        block = part * 2 + below
        ref[at : at + SLICE, block * 128 : (block + 1) * 128] = value[
            below * SLICE : (below + 1) * SLICE, :
        ]
    if part == 1:
        ref[at : at + 6, LAT:LATW] = value[24:30, 0:64]
        ref[at + 6 : at + 12, LAT:LATW] = value[24:30, 64:128]


def kernel(
    q_hbm, g_hbm, lat_hbm, ids_hbm, node_ref, ids_ref, len_ref,
    att_hbm, node_out, own_out,
    qb, gb, kb, kf, dk, pk, pbt, dst, att,
    ids_all,
    col_a, col_b, xs, xr_a, xr_b, zs, zr, zs2, zr2, xs2, xr2, ys, yr,
    os_, or_, ag,
    sem_local, sem_q, sem_att, sem_ids, sem_y, sem_x, sem_z, sem_z2, sem_x2, sem_y2, sem_o, sem_ag, sem_fin,
):
    zlo, x, y, zhi, core = place()
    other = 1 - core
    half = qb.shape[0] // 2
    own_rows = kb.shape[0] - kf.shape[0]
    columns = ZLO * YS
    col, xr = (col_a, col_b), (xr_a, xr_b)

    def remote(src, dst_, sems, index, where):
        return pltpu.make_async_remote_copy(
            src_ref=src, dst_ref=dst_, send_sem=sems.at[(0, *index)], recv_sem=sems.at[(1, *index)],
            device_id=where, device_id_type=MESH,
        )

    def column_peer(k):
        return device(lax.rem(zlo + k // YS, ZLO), x, lax.rem(y + k % YS, YS), zhi, core)

    def x_peer(o, c):
        return device(zlo, lax.rem(x + o, XS), y, zhi, lax.rem(core + c, 2))

    def z_peer(o):
        return device(zlo, x, y, lax.rem(zhi + o, ZHI), core)

    x_moves = [(o, c) for o in range(XS) for c in range(2) if o or c]

    barrier = pltpu.get_barrier_semaphore()

    @pl.loop(1, columns)
    def _(k):
        pl.semaphore_signal(barrier, inc=1, device_id=column_peer(k), device_id_type=MESH)

    for o, c in x_moves:
        pl.semaphore_signal(barrier, inc=1, device_id=x_peer(o, c), device_id_type=MESH)
    for o in range(1, ZHI):
        pl.semaphore_signal(barrier, inc=1, device_id=z_peer(o), device_id_type=MESH)

    locals_in = [
        pltpu.make_async_copy(q_hbm.at[pl.ds(core * half, half)], qb.at[pl.ds(0, half)], sem_local.at[0]),
        pltpu.make_async_copy(g_hbm.at[pl.ds(core * half, half)], gb.at[pl.ds(0, half)], sem_local.at[1]),
        pltpu.make_async_copy(
            lat_hbm.at[pl.ds(core * own_rows, own_rows)], kb.at[pl.ds(kf.shape[0], own_rows)], sem_local.at[2]
        ),
    ]
    for copy in locals_in:
        copy.start()

    mine = zlo * YS + y
    pk[0, :, 0:UNIT, :] = jnp.zeros((2, UNIT, 128), F32)
    pack(node_ref[...].astype(F32), pk.at[0], 0)
    for part in range(2):
        col[part][mine] = pk[0, part, 0:UNIT, :].astype(BF16)
    for leaf in range(2):
        for s in range(3):
            ids_all[0, leaf, s] = ids_ref[leaf, s]

    pl.semaphore_wait(barrier, columns - 1 + len(x_moves) + ZHI - 1)

    def ids_copy(o):
        return remote(ids_hbm, ids_all.at[o], sem_ids, (o,), x_peer(o, 0))

    def y_copy(part, k):
        return remote(col[part].at[mine], col[part].at[mine], sem_y, (part, k), column_peer(k))

    for o in range(1, XS):
        ids_copy(o).start()
    for part in range(2):

        @pl.loop(1, columns)
        def _(k):
            y_copy(part, k).start()

    swap = [
        remote(q_hbm.at[pl.ds(other * half, half)], qb.at[pl.ds(half, half)], sem_q, (0,), x_peer(0, 1)),
        remote(g_hbm.at[pl.ds(other * half, half)], gb.at[pl.ds(half, half)], sem_q, (1,), x_peer(0, 1)),
    ]
    for copy in swap:
        copy.start()

    for o in range(1, XS):
        ids_copy(o).wait()

    def x_copy(part, o, c):
        return remote(xs.at[part, o, c], xr[part].at[o, c], sem_x, (part, o, c), x_peer(o, c))

    def column_of(node):
        return (node // (XS * YS)) * YS + node % YS

    for part in range(2):

        @pl.loop(1, columns)
        def _(k):
            y_copy(part, k).wait_recv()

        for o in range(XS):
            for c in range(2):
                leaf = lax.rem(core + c, 2)
                for s in range(3):
                    node = ids_all[(XS - o) % XS, leaf, s]
                    piece = col[part][column_of(node)]
                    if o or c:
                        xs[part, o, c, s * UNIT : (s + 1) * UNIT, :] = piece
                    else:
                        xr[part][o, c, s * UNIT : (s + 1) * UNIT, :] = piece
        for o, c in x_moves:
            x_copy(part, o, c).start()

    def z_copy(part, o):
        return remote(zs.at[part], zr.at[part, o], sem_z, (part, o), z_peer(o))

    for part in range(2):
        for o, c in x_moves:
            x_copy(part, o, c).wait_recv()
        for s in range(3):
            from_x = (ids_all[0, core, s] // YS) % XS
            o = lax.rem(x - from_x + XS, XS)
            for c in range(2):
                at = (c * 3 + s) * UNIT
                zs[part, at : at + UNIT, :] = xr[part][o, c, s * UNIT : (s + 1) * UNIT, :]
        for o in range(1, ZHI):
            z_copy(part, o).start()

    def keys_from(part, o, block):
        for u in range(6):
            unpack(part, block[u * UNIT : (u + 1) * UNIT, :], kf, (o * 6 + u) * SLICE)

    for part in range(2):
        keys_from(part, 0, zs[part].astype(F32))
    for part in range(2):
        for o in range(1, ZHI):
            z_copy(part, o).wait_recv()
            keys_from(part, o, zr[part, o].astype(F32))
    node_keys = kf.shape[0]
    for copy in locals_in:
        copy.wait()
    for copy in swap:
        copy.wait()
    kb[0:node_keys, :] = kf[...].astype(BF16)

    length = len_ref[core]
    heads = half // own_rows
    step = min(256, half)

    @pl.loop(0, 2 * half // step)
    def _(b):
        at = pl.multiple_of(b * step, step)
        first = lax.rem(b * step, half)
        query = qb[pl.ds(at, step), :]
        keys = kb[...]
        values = keys[:, :LAT]
        scores = lax.dot_general(keys, query, (((1,), (1,)), ((), ())), preferred_element_type=F32) * score_scale
        row = (first + lax.broadcasted_iota(jnp.int32, (own_rows, step), 1)) // heads
        seen = lax.broadcasted_iota(jnp.int32, (own_rows, step), 0) <= row
        scores = jnp.concatenate(
            [scores[:node_keys], jnp.where(seen, scores[node_keys:], -jnp.inf)], axis=0
        )
        top = jnp.max(scores, axis=0, keepdims=True)
        expo = jnp.exp(scores - top)
        probs = expo * (1.0 / jnp.sum(expo, axis=0, keepdims=True))
        probs_b = probs.astype(BF16)
        live = (first + lax.broadcasted_iota(jnp.int32, (step, LAT), 0)) // heads < length
        masked = jnp.where(live, gb[pl.ds(at, step), :].astype(F32), 0.0).astype(BF16)
        gb[pl.ds(at, step), :] = masked
        dprobs = lax.dot_general(values, masked, (((1,), (1,)), ((), ())), preferred_element_type=F32)
        delta = jnp.sum(probs_b.astype(F32) * dprobs, axis=0, keepdims=True)
        pbt[:, pl.ds(at, step)] = probs_b
        dst[:, pl.ds(at, step)] = (score_scale * probs * (dprobs - delta)).astype(BF16)
        outputs = lax.dot_general(probs_b, values, (((0,), (0,)), ((), ())), preferred_element_type=F32)
        att[pl.ds(at, step), :] = jnp.where(live, outputs, 0.0).astype(BF16)

    att_local = pltpu.make_async_copy(att.at[pl.ds(0, half)], att_hbm.at[pl.ds(core * half, half)], sem_local.at[0])
    att_swap = remote(att.at[pl.ds(half, half)], att_hbm.at[pl.ds(core * half, half)], sem_att, (), x_peer(0, 1))
    att_local.start()
    att_swap.start()

    dk[...] = lax.dot_general(dst[...], qb[...], (((1,), (0,)), ((), ())), preferred_element_type=F32)
    dk[:, :LAT] += lax.dot_general(pbt[...], gb[...], (((1,), (0,)), ((), ())), preferred_element_type=F32)

    def z2_copy(part, o):
        return remote(zs2.at[part, o], zr2.at[part, o], sem_z2, (part, o), z_peer(o))

    for o in range(ZHI):
        back = (ZHI - o) % ZHI
        for u in range(6):
            at = (o * 6 + u) * SLICE
            pack(dk[at : at + SLICE, :], pk.at[back], u * UNIT)
        if back:
            for part in range(2):
                zs2[part, back] = pk[back, part].astype(BF16)
                z2_copy(part, back).start()

    quarter = own_rows // ZHI

    def o_copy(o):
        return remote(os_.at[o], or_.at[o], sem_o, (o,), z_peer(o))

    for o in range(1, ZHI):
        at = pl.multiple_of(node_keys + lax.rem(zhi + o, ZHI) * quarter, quarter)
        os_[o] = dk[pl.ds(at, quarter), :].astype(BF16)
        o_copy(o).start()

    def x2_copy(part, o, c):
        return remote(xs2.at[part, c], xr2.at[part, o, c], sem_x2, (part, o, c), x_peer(o, c))

    for part in range(2):
        total = pk[0, part]
        for o in range(1, ZHI):
            z2_copy(part, o).wait_recv()
            total = total + zr2[part, o].astype(F32)
        total = total.astype(BF16)
        for c in range(2):
            block = total[c * 3 * UNIT : (c + 1) * 3 * UNIT, :]
            xs2[part, c] = block
        xr2[part, 0, 0] = xs2[part, 0]
        for o, c in x_moves:
            x2_copy(part, o, c).start()

    def ag_copy(o):
        return remote(ag.at[0], ag.at[o], sem_ag, (o,), z_peer(o))

    at = pl.multiple_of(node_keys + zhi * quarter, quarter)
    total = dk[pl.ds(at, quarter), :]
    for o in range(1, ZHI):
        o_copy(o).wait_recv()
        total = total + or_[o].astype(F32)
    ag[0] = total.astype(BF16)
    for o in range(1, ZHI):
        ag_copy(o).start()

    def y2_copy(part, k):
        to = lax.rem(zlo + k // YS, ZLO) * YS + lax.rem(y + k % YS, YS)
        return remote(ys.at[part, to], yr.at[part, k], sem_y2, (part, k), column_peer(k))

    for part in range(2):
        for o, c in x_moves:
            x2_copy(part, o, c).wait_recv()

        @pl.loop(0, columns)
        def _(t):
            target = ((t // YS) * XS + x) * YS + t % YS
            acc = jnp.zeros((UNIT, 128), F32)
            for o in range(XS):
                for c in range(2):
                    leaf = lax.rem(core + c, 2)
                    for s in range(3):
                        node = ids_all[o, leaf, s]
                        hit = jnp.where(node == target, 1.0, 0.0).astype(F32)
                        acc = acc + hit * xr2[part, o, c, s * UNIT : (s + 1) * UNIT, :].astype(F32)
            ys[part, t] = acc.astype(BF16)

        @pl.loop(1, columns)
        def _(k):
            y2_copy(part, k).start()

    for o in range(1, ZHI):
        ag_copy(o).wait_recv()
    for o in range(ZHI):
        origin = lax.rem(zhi - o + ZHI, ZHI)
        own_out[core, pl.ds(pl.multiple_of(origin * quarter, quarter), quarter), :] = ag[o]
    fin = remote(own_out.at[core], own_out.at[core], sem_fin, (), x_peer(0, 1))
    fin.start()

    for part in range(2):
        total = ys[part, mine].astype(F32)

        for k in range(1, columns):
            y2_copy(part, k).wait_recv()
            total = total + yr[part, k].astype(F32)
        unpack(part, total, dk, 0)
    node_out[...] = dk[0:SLICE, :].astype(BF16)

    for part in range(2):

        @pl.loop(1, columns)
        def _(k):
            y_copy(part, k).wait_send()
            y2_copy(part, k).wait_send()

        for o, c in x_moves:
            x_copy(part, o, c).wait_send()
            x2_copy(part, o, c).wait_send()
        for o in range(1, ZHI):
            z_copy(part, o).wait_send()
            z2_copy(part, o).wait_send()
    for o in range(1, ZHI):
        o_copy(o).wait_send()
        ag_copy(o).wait_send()
    fin.wait()
    att_local.wait()
    att_swap.wait()


def body(queries, leaf_latent, node_latent, grad_out, leaf_nodes, leaf_lengths):
    rows, heads, width = queries.shape
    total = rows * heads
    own_rows = rows // 2
    node_keys = ZHI * 6 * SLICE
    keys = node_keys + own_rows
    columns = ZLO * YS
    vmem = pl.BlockSpec(memory_space=pltpu.VMEM)
    smem = pl.BlockSpec(memory_space=pltpu.SMEM)
    hbm = pl.BlockSpec(memory_space=pl.ANY)
    dma = pltpu.SemaphoreType.DMA
    flops = 2 * total * keys * (3 * LAT + 2 * LATW)
    att, node_grad, own = pl.pallas_call(
        kernel,
        out_shape=(
            jax.ShapeDtypeStruct((total, LAT), BF16),
            jax.ShapeDtypeStruct((SLICE, width), BF16),
            jax.ShapeDtypeStruct((2, own_rows, width), BF16),
        ),
        in_specs=[hbm, hbm, hbm, hbm, vmem, smem, smem],
        out_specs=(hbm, vmem, vmem),
        scratch_shapes=[
            pltpu.VMEM((total, width), BF16),
            pltpu.VMEM((total, LAT), BF16),
            pltpu.VMEM((keys, width), BF16),
            pltpu.VMEM((node_keys, width), F32),
            pltpu.VMEM((keys, width), F32),
            pltpu.VMEM((ZHI, 2, 6 * UNIT, 128), F32),
            pltpu.VMEM((keys, total), BF16),
            pltpu.VMEM((keys, total), BF16),
            pltpu.VMEM((total, LAT), BF16),
            pltpu.SMEM((XS, 2, 3), jnp.int32),
            pltpu.VMEM((columns, UNIT, 128), BF16),
            pltpu.VMEM((columns, UNIT, 128), BF16),
            pltpu.VMEM((2, XS, 2, 3 * UNIT, 128), BF16),
            pltpu.VMEM((XS, 2, 3 * UNIT, 128), BF16),
            pltpu.VMEM((XS, 2, 3 * UNIT, 128), BF16),
            pltpu.VMEM((2, 6 * UNIT, 128), BF16),
            pltpu.VMEM((2, ZHI, 6 * UNIT, 128), BF16),
            pltpu.VMEM((2, ZHI, 6 * UNIT, 128), BF16),
            pltpu.VMEM((2, ZHI, 6 * UNIT, 128), BF16),
            pltpu.VMEM((2, 2, 3 * UNIT, 128), BF16),
            pltpu.VMEM((2, XS, 2, 3 * UNIT, 128), BF16),
            pltpu.VMEM((2, columns, UNIT, 128), BF16),
            pltpu.VMEM((2, columns, UNIT, 128), BF16),
            pltpu.VMEM((ZHI, own_rows // ZHI, width), BF16),
            pltpu.VMEM((ZHI, own_rows // ZHI, width), BF16),
            pltpu.VMEM((ZHI, own_rows // ZHI, width), BF16),
            dma((3,)),
            dma((2, 2)),
            dma((2,)),
            dma((2, XS)),
            dma((2, 2, columns)),
            dma((2, 2, XS, 2)),
            dma((2, 2, ZHI)),
            dma((2, 2, ZHI)),
            dma((2, 2, XS, 2)),
            dma((2, 2, columns)),
            dma((2, ZHI)),
            dma((2, ZHI)),
            dma((2,)),
        ],
        compiler_params=pltpu.CompilerParams(
            collective_id=0, has_side_effects=True, vmem_limit_bytes=48 * 2**20
        ),
        cost_estimate=pl.CostEstimate(
            flops=flops, bytes_accessed=2 * total * (width + 2 * LAT), transcendentals=total * keys
        ),
        name="leaves",
    )(
        queries.reshape(total, width),
        grad_out.reshape(total, LAT),
        leaf_latent,
        leaf_nodes,
        node_latent.reshape(SLICE, width),
        leaf_nodes,
        leaf_lengths,
    )
    return (
        att.reshape(rows, heads, LAT),
        node_grad.reshape(node_latent.shape),
        own.reshape(rows, width),
    )


def solution(mesh):
    return jax.shard_map(
        body,
        mesh=mesh,
        in_specs=(
            P("leaf", "head", None),
            P("leaf", None),
            P("leaf", "head", None),
            P("leaf", "head", None),
            P("leaf", None),
            P("leaf"),
        ),
        out_specs=(P("leaf", "head", None), P("leaf", "head", None), P("leaf", None)),
        check_vma=False,
    )
```

```python
import functools

import jax
import jax.numpy as jnp
from jax import lax
from jax.experimental import pallas as pl
from jax.experimental.pallas import tpu as pltpu
from jax.sharding import PartitionSpec as P

MESH = pl.DeviceIdType.MESH
ZLO, XS, YS, ZHI = 2, 4, 8, 4
LAT = 512
LATW = 576
SLICE = 12
HALF = 6
UNIT = 32
score_scale = 192.0 ** (-0.5)
F32 = jnp.float32
BF16 = jnp.bfloat16


def place():
    leaf, head = lax.axis_index("leaf"), lax.axis_index("head")
    return leaf // (XS * YS), (leaf // YS) % XS, leaf % YS, head // 2, head % 2


def device(zlo, x, y, zhi, core):
    return ((zlo * XS + x) * YS + y, zhi * 2 + core)


def pack(rows, ref, at):
    for block in range(4):
        ref[at + block * HALF : at + (block + 1) * HALF, :] = rows[:, block * 128 : (block + 1) * 128]
    ref[at + 24 : at + 27, :] = jnp.concatenate([rows[0:3, LAT:LATW], rows[3:6, LAT:LATW]], axis=1)


def unpack(value, ref, at):
    for block in range(4):
        ref[at : at + HALF, block * 128 : (block + 1) * 128] = value[block * HALF : (block + 1) * HALF, :]
    ref[at : at + 3, LAT:LATW] = value[24:27, 0:64]
    ref[at + 3 : at + 6, LAT:LATW] = value[24:27, 64:128]


def kernel(
    q_hbm, g_hbm, lat_hbm, ids_hbm, node_hbm, ids_ref, len_ref,
    att_hbm, node_out, own_out,
    qt, qf, qs, qb, gb, lt, lf, nd, kb, kf, sc, dp, dk, pk, pbt, dst, att,
    ids_all, pick,
    col_a, col_b, xs, xr_a, xr_b, zs, zr, zs2, zr2, xs2, xr2, ys, yr,
    os_, or_, ag,
    sem_local, sem_q, sem_att, sem_ids, sem_y, sem_x, sem_z, sem_z2, sem_x2, sem_y2, sem_o, sem_ag, sem_fin,
):
    zlo, x, y, zhi, core = place()
    other = 1 - core
    half = qb.shape[0] // 2
    heads = qt.shape[0]
    node_keys = kf.shape[0]
    part_keys = node_keys // 2
    own_rows = kb.shape[0] - node_keys
    columns = ZLO * YS
    col, xr = (col_a, col_b), (xr_a, xr_b)

    def remote(src, dst_, sems, index, where):
        return pltpu.make_async_remote_copy(
            src_ref=src, dst_ref=dst_, send_sem=sems.at[(0, *index)], recv_sem=sems.at[(1, *index)],
            device_id=where, device_id_type=MESH,
        )

    def column_place(k, sign):
        turn = k // ZLO
        along = YS // 2 + ((turn + 1) // 2) * (1 - 2 * (turn % 2))
        across = ZLO - 1 - k % ZLO
        return (zlo + sign * across + ZLO) % ZLO, (y + sign * along + YS) % YS

    def column_peer(k):
        a, b = column_place(k, 1)
        return device(a, x, b, zhi, core)

    def x_peer(o, c):
        return device(zlo, lax.rem(x + o, XS), y, zhi, lax.rem(core + c, 2))

    def z_peer(o):
        return device(zlo, x, y, lax.rem(zhi + o, ZHI), core)

    x_moves = [(o, c) for o in range(XS) for c in range(2) if o or c]
    node_in = pltpu.make_async_copy(node_hbm, nd, sem_local.at[0])
    node_in.start()

    barrier = pltpu.get_barrier_semaphore()

    @pl.loop(0, columns - 1)
    def _(k):
        pl.semaphore_signal(barrier, inc=1, device_id=column_peer(k), device_id_type=MESH)

    for o, c in x_moves:
        pl.semaphore_signal(barrier, inc=1, device_id=x_peer(o, c), device_id_type=MESH)
    for o in range(1, ZHI):
        pl.semaphore_signal(barrier, inc=1, device_id=z_peer(o), device_id_type=MESH)

    q_in = pltpu.make_async_copy(q_hbm, qt, sem_local.at[1])
    g_in = pltpu.make_async_copy(g_hbm.at[pl.ds(core * half, half)], gb.at[pl.ds(0, half)], sem_local.at[2])
    lat_in = pltpu.make_async_copy(lat_hbm, lt, sem_local.at[3])
    q_in.start()
    g_in.start()
    lat_in.start()

    mine = zlo * YS + y
    for leaf in range(2):
        for s in range(3):
            ids_all[0, leaf, s] = ids_ref[leaf, s]
    pk[0, :, 0:UNIT, :] = jnp.zeros((2, UNIT, 128), F32)
    node_in.wait()
    slice_rows = nd[...].astype(F32)
    for part in range(2):
        pack(slice_rows[part * HALF : (part + 1) * HALF, :], pk.at[0, part], 0)
        col[part][mine] = pk[0, part, 0:UNIT, :].astype(BF16)

    pl.semaphore_wait(barrier, columns - 1 + len(x_moves) + ZHI - 1)

    def ids_copy(o):
        return remote(ids_hbm, ids_all.at[o], sem_ids, (o,), x_peer(o, 0))

    def y_copy(part, k):
        return remote(col[part].at[mine], col[part].at[mine], sem_y, (part, k), column_peer(k))

    for part in range(2):

        @pl.loop(0, columns - 1)
        def _(k):
            y_copy(part, k).start()

        if part == 0:
            for o in range(1, XS):
                ids_copy(o).start()

    g_swap = remote(g_hbm.at[pl.ds(other * half, half)], gb.at[pl.ds(half, half)], sem_q, (1,), x_peer(0, 1))
    g_swap.start()

    q_in.wait()

    @pl.loop(0, heads)
    def _(h):
        for block in range(5):
            piece = qt[h, block * 128 : min((block + 1) * 128, LATW), :].astype(F32)
            if block == 4:
                piece = jnp.concatenate([piece, jnp.zeros((64, piece.shape[1]), F32)], axis=0)
            qf[block, pl.ds(h, 2 * own_rows, stride=heads), :] = jnp.transpose(piece)

    for block in range(5):
        to = slice(block * 128, min((block + 1) * 128, LATW))
        for leaf_of, rows_to in ((core, qb), (other, qs)):
            piece = qf[block, pl.ds(pl.multiple_of(leaf_of * half, half), half), :].astype(BF16)
            rows_to[0:half, to] = piece[:, : to.stop - to.start]
    q_swap = remote(qs, qb.at[pl.ds(half, half)], sem_q, (0,), x_peer(0, 1))
    q_swap.start()

    for o in range(1, XS):
        ids_copy(o).wait()

    def x_copy(part, o, c):
        return remote(xs.at[part, o, c], xr[part].at[o, c], sem_x, (part, o, c), x_peer(o, c))

    def column_of(node):
        return (node // (XS * YS)) * YS + node % YS

    for part in range(2):

        @pl.loop(0, columns - 1)
        def _(k):
            y_copy(part, k).wait_recv()

        for o in reversed(range(XS)):
            for c in range(2):
                leaf = lax.rem(core + c, 2)
                for s in range(3):
                    node = ids_all[(XS - o) % XS, leaf, s]
                    piece = col[part][column_of(node)]
                    if o or c:
                        xs[part, o, c, s * UNIT : (s + 1) * UNIT, :] = piece
                    else:
                        xr[part][o, c, s * UNIT : (s + 1) * UNIT, :] = piece
                if o or c:
                    x_copy(part, o, c).start()

    lat_in.wait()
    lf[...] = jnp.transpose(lt[...].astype(F32))
    kb[node_keys:, :] = lf[pl.ds(pl.multiple_of(core * own_rows, own_rows), own_rows), :].astype(BF16)

    def z_copy(part, o):
        return remote(zs.at[part], zr.at[part, o], sem_z, (part, o), z_peer(o))

    for part in range(2):
        for o, c in x_moves:
            x_copy(part, o, c).wait_recv()
        for s in range(3):
            from_x = (ids_all[0, core, s] // YS) % XS
            o = lax.rem(x - from_x + XS, XS)
            for c in range(2):
                at = (c * 3 + s) * UNIT
                zs[part, at : at + UNIT, :] = xr[part][o, c, s * UNIT : (s + 1) * UNIT, :]
        for o in (2, 1, 3):
            if o < ZHI:
                z_copy(part, o).start()

    def unpack_keys(part, o, block):
        for u in range(6):
            unpack(block[u * UNIT : (u + 1) * UNIT, :], kf, part * part_keys + (o * 6 + u) * HALF)

    def products(at, count):
        keys = kb[at : at + count, :]
        sc[at : at + count, :] = score_scale * lax.dot_general(
            keys, qb[...], (((1,), (1,)), ((), ())), preferred_element_type=F32
        )
        dp[at : at + count, :] = lax.dot_general(
            keys[:, :LAT], gb[...], (((1,), (1,)), ((), ())), preferred_element_type=F32
        )

    length = len_ref[core]
    g_in.wait()
    g_swap.wait()
    q_swap.wait()
    step = min(256, half)

    def live_rows(at):
        first = lax.rem(at, half)
        return (first + lax.broadcasted_iota(jnp.int32, (step, LAT), 0)) // heads < length

    @pl.loop(0, 2 * half // step)
    def _(b):
        at = pl.multiple_of(b * step, step)
        gb[pl.ds(at, step), :] = jnp.where(live_rows(at), gb[pl.ds(at, step), :].astype(F32), 0.0).astype(BF16)

    products(node_keys, own_rows)
    for part in range(2):
        unpack_keys(part, 0, zs[part].astype(F32))
    pk[...] = jnp.zeros(pk.shape, F32)
    for part in range(2):
        for o in (1, 3, 2):
            if o < ZHI:
                z_copy(part, o).wait_recv()
                unpack_keys(part, o, zr[part, o].astype(F32))
        at = part * part_keys
        kb[at : at + part_keys, :] = kf[at : at + part_keys, :].astype(BF16)
        products(at, part_keys)

    @pl.loop(0, 2 * half // step)
    def _(b):
        at = pl.multiple_of(b * step, step)
        first = lax.rem(b * step, half)
        row = (first + lax.broadcasted_iota(jnp.int32, (own_rows, step), 1)) // heads
        seen = lax.broadcasted_iota(jnp.int32, (own_rows, step), 0) <= row
        scores = jnp.concatenate(
            [sc[0:node_keys, pl.ds(at, step)], jnp.where(seen, sc[node_keys:, pl.ds(at, step)], -jnp.inf)], axis=0
        )
        dprobs = dp[:, pl.ds(at, step)]
        top = jnp.max(scores, axis=0, keepdims=True)
        expo = jnp.exp(scores - top)
        probs = expo * (1.0 / jnp.sum(expo, axis=0, keepdims=True))
        probs_b = probs.astype(BF16)
        delta = jnp.sum(probs_b.astype(F32) * dprobs, axis=0, keepdims=True)
        pbt[:, pl.ds(at, step)] = probs_b
        dst[:, pl.ds(at, step)] = (score_scale * probs * (dprobs - delta)).astype(BF16)

    def z2_copy(part, o):
        return remote(zs2.at[part, o], zr2.at[part, o], sem_z2, (part, o), z_peer(o))

    def key_terms(at, count):
        dk[at : at + count, :] = lax.dot_general(
            dst[at : at + count, :], qb[...], (((1,), (0,)), ((), ())), preferred_element_type=F32
        )
        dk[at : at + count, :LAT] += lax.dot_general(
            pbt[at : at + count, :], gb[...], (((1,), (0,)), ((), ())), preferred_element_type=F32
        )

    for part in range(2):
        key_terms(part * part_keys, part_keys)
        for o in (2, 1, 3, 0):
            if o < ZHI:
                back = (ZHI - o) % ZHI
                for u in range(6):
                    at = part * part_keys + (o * 6 + u) * HALF
                    pack(dk[at : at + HALF, :], pk.at[back, part], u * UNIT)
                if back:
                    zs2[part, back] = pk[back, part].astype(BF16)
                    z2_copy(part, back).start()
    key_terms(node_keys, own_rows)

    quarter = own_rows // ZHI

    def o_copy(o):
        return remote(os_.at[o], or_.at[o], sem_o, (o,), z_peer(o))

    for o in range(1, ZHI):
        at = pl.multiple_of(node_keys + lax.rem(zhi + o, ZHI) * quarter, quarter)
        os_[o] = dk[pl.ds(at, quarter), :].astype(BF16)
        o_copy(o).start()

    for group in range(pick.shape[1] // 128):
        lane = lax.broadcasted_iota(jnp.int32, pick.shape[:1] + (128,), 1)
        line = lax.broadcasted_iota(jnp.int32, pick.shape[:1] + (128,), 0)
        goal = jnp.full(lane.shape, -1, jnp.int32)
        for quad in range(4):
            term = group * 4 + quad
            o, c, s = term // 6, (term // 3) % 2, term % 3
            node = ids_all[o, lax.rem(core + c, 2), s]
            place_ = jnp.where((node // YS) % XS == x, column_of(node), -1)
            goal = jnp.where(lane // UNIT == quad, place_, goal)
        hit = (line // UNIT == goal) & (line % UNIT == lane % UNIT)
        pick[:, group * 128 : (group + 1) * 128] = jnp.where(hit, 1.0, 0.0).astype(BF16)

    @pl.loop(0, 2 * half // step)
    def _(b):
        at = pl.multiple_of(b * step, step)
        outputs = lax.dot_general(
            pbt[:, pl.ds(at, step)], kb[:, :LAT], (((0,), (0,)), ((), ())), preferred_element_type=F32
        )
        att[pl.ds(at, step), :] = jnp.where(live_rows(at), outputs, 0.0).astype(BF16)

    att_local = pltpu.make_async_copy(att.at[pl.ds(0, half)], att_hbm.at[pl.ds(core * half, half)], sem_local.at[4])
    att_swap = remote(att.at[pl.ds(half, half)], att_hbm.at[pl.ds(core * half, half)], sem_att, (), x_peer(0, 1))
    att_local.start()
    att_swap.start()

    def x2_copy(part, o, c):
        return remote(xs2.at[part, c], xr2.at[part, o, c], sem_x2, (part, o, c), x_peer(o, c))

    for part in range(2):
        total = pk[0, part]
        for o in range(1, ZHI):
            z2_copy(part, o).wait_recv()
            total = total + zr2[part, o].astype(F32)
        total = total.astype(BF16)
        for c in range(2):
            xs2[part, c] = total[c * 3 * UNIT : (c + 1) * 3 * UNIT, :]
        xr2[part, 0, 0] = total[0 : 3 * UNIT, :]
        for o, c in reversed(x_moves):
            x2_copy(part, o, c).start()

    def ag_copy(o):
        return remote(ag.at[0], ag.at[o], sem_ag, (o,), z_peer(o))

    at = pl.multiple_of(node_keys + zhi * quarter, quarter)
    total = dk[pl.ds(at, quarter), :]
    for o in range(1, ZHI):
        o_copy(o).wait_recv()
        total = total + or_[o].astype(F32)
    ag[0] = total.astype(BF16)
    for o in range(1, ZHI):
        ag_copy(o).start()

    def y2_copy(part, k):
        a, b = column_place(k, 1)
        return remote(ys.at[part, a * YS + b], yr.at[part, k], sem_y2, (part, k), column_peer(k))

    for part in range(2):
        for o, c in x_moves:
            x2_copy(part, o, c).wait_recv()
        terms = xr2[part].reshape(XS * 2 * 3 * UNIT, 128)
        sums = jnp.dot(pick[...], terms, preferred_element_type=F32)
        ys[part] = sums.astype(BF16).reshape(columns, UNIT, 128)

        @pl.loop(0, columns - 1)
        def _(k):
            y2_copy(part, k).start()

    for o in range(1, ZHI):
        ag_copy(o).wait_recv()
    for o in range(ZHI):
        origin = lax.rem(zhi - o + ZHI, ZHI)
        own_out[core, pl.ds(pl.multiple_of(origin * quarter, quarter), quarter), :] = ag[o]
    fin = remote(own_out.at[core], own_out.at[core], sem_fin, (), x_peer(0, 1))
    fin.start()

    for part in range(2):

        @pl.loop(0, columns - 1)
        def _(k):
            y_copy(part, k).wait_send()

        for o, c in x_moves:
            x_copy(part, o, c).wait_send()
            x2_copy(part, o, c).wait_send()
        for o in range(1, ZHI):
            z_copy(part, o).wait_send()
            z2_copy(part, o).wait_send()
    for o in range(1, ZHI):
        o_copy(o).wait_send()
        ag_copy(o).wait_send()
    att_local.wait()
    att_swap.wait()

    for part in range(2):
        for k in range(columns - 1):
            y2_copy(part, k).wait_recv()
        total = ys[part, mine].astype(F32)
        for k in range(columns - 1):
            total = total + yr[part, k].astype(F32)
        unpack(total, dk, part * HALF)
    node_out[...] = dk[0:SLICE, :].astype(BF16)
    fin.wait()
    for part in range(2):

        @pl.loop(0, columns - 1)
        def _(k):
            y2_copy(part, k).wait_send()


def body(queries, leaf_latent, node_latent, grad_out, leaf_nodes, leaf_lengths):
    rows, heads, width = queries.shape
    total = rows * heads
    own_rows = rows // 2
    node_keys = ZHI * 6 * SLICE
    keys = node_keys + own_rows
    columns = ZLO * YS
    vmem = pl.BlockSpec(memory_space=pltpu.VMEM)
    smem = pl.BlockSpec(memory_space=pltpu.SMEM)
    hbm = pl.BlockSpec(memory_space=pl.ANY)
    dma = pltpu.SemaphoreType.DMA
    flops = 2 * total * keys * (3 * LAT + 2 * LATW)
    att, node_grad, own = pl.pallas_call(
        kernel,
        out_shape=(
            pltpu.VMEM((total, LAT), BF16),
            pltpu.VMEM((SLICE, width), BF16),
            pltpu.VMEM((2, own_rows, width), BF16),
        ),
        in_specs=[hbm, hbm, hbm, hbm, hbm, smem, smem],
        out_specs=(hbm, vmem, vmem),
        scratch_shapes=[
            pltpu.VMEM((heads, width, rows), BF16),
            pltpu.VMEM((5, total, 128), F32),
            pltpu.VMEM((total // 2, width), BF16),
            pltpu.VMEM((total, width), BF16),
            pltpu.VMEM((total, LAT), BF16),
            pltpu.VMEM((width, rows), BF16),
            pltpu.VMEM((rows, width), F32),
            pltpu.VMEM((SLICE, width), BF16),
            pltpu.VMEM((keys, width), BF16),
            pltpu.VMEM((node_keys, width), F32),
            pltpu.VMEM((keys, total), F32),
            pltpu.VMEM((keys, total), F32),
            pltpu.VMEM((keys, width), F32),
            pltpu.VMEM((ZHI, 2, 6 * UNIT, 128), F32),
            pltpu.VMEM((keys, total), BF16),
            pltpu.VMEM((keys, total), BF16),
            pltpu.VMEM((total, LAT), BF16),
            pltpu.SMEM((XS, 2, 3), jnp.int32),
            pltpu.VMEM((columns * UNIT, XS * 6 * UNIT), BF16),
            pltpu.VMEM((columns, UNIT, 128), BF16),
            pltpu.VMEM((columns, UNIT, 128), BF16),
            pltpu.VMEM((2, XS, 2, 3 * UNIT, 128), BF16),
            pltpu.VMEM((XS, 2, 3 * UNIT, 128), BF16),
            pltpu.VMEM((XS, 2, 3 * UNIT, 128), BF16),
            pltpu.VMEM((2, 6 * UNIT, 128), BF16),
            pltpu.VMEM((2, ZHI, 6 * UNIT, 128), BF16),
            pltpu.VMEM((2, ZHI, 6 * UNIT, 128), BF16),
            pltpu.VMEM((2, ZHI, 6 * UNIT, 128), BF16),
            pltpu.VMEM((2, 2, 3 * UNIT, 128), BF16),
            pltpu.VMEM((2, XS, 2, 3 * UNIT, 128), BF16),
            pltpu.VMEM((2, columns, UNIT, 128), BF16),
            pltpu.VMEM((2, columns, UNIT, 128), BF16),
            pltpu.VMEM((ZHI, own_rows // ZHI, width), BF16),
            pltpu.VMEM((ZHI, own_rows // ZHI, width), BF16),
            pltpu.VMEM((ZHI, own_rows // ZHI, width), BF16),
            dma((5,)),
            dma((2, 2)),
            dma((2,)),
            dma((2, XS)),
            dma((2, 2, columns)),
            dma((2, 2, XS, 2)),
            dma((2, 2, ZHI)),
            dma((2, 2, ZHI)),
            dma((2, 2, XS, 2)),
            dma((2, 2, columns)),
            dma((2, ZHI)),
            dma((2, ZHI)),
            dma((2,)),
        ],
        compiler_params=pltpu.CompilerParams(
            collective_id=0, has_side_effects=True, vmem_limit_bytes=61 * 2**20
        ),
        cost_estimate=pl.CostEstimate(
            flops=flops, bytes_accessed=2 * total * (width + 2 * LAT), transcendentals=total * keys
        ),
        name="leaves",
    )(
        queries.transpose(1, 2, 0),
        grad_out.reshape(total, LAT),
        leaf_latent.T,
        leaf_nodes,
        node_latent.reshape(SLICE, width),
        leaf_nodes,
        leaf_lengths,
    )
    return (
        att.reshape(rows, heads, LAT),
        node_grad.reshape(node_latent.shape),
        own.reshape(rows, width),
    )


def solution(mesh):
    return jax.shard_map(
        body,
        mesh=mesh,
        in_specs=(
            P("leaf", "head", None),
            P("leaf", None),
            P("leaf", "head", None),
            P("leaf", "head", None),
            P("leaf", None),
            P("leaf"),
        ),
        out_specs=(P("leaf", "head", None), P("leaf", "head", None), P("leaf", None)),
        check_vma=False,
    )
```

```python
import functools

import jax
import jax.numpy as jnp
from jax import lax
from jax.experimental import pallas as pl
from jax.experimental.pallas import tpu as pltpu
from jax.sharding import PartitionSpec as P

MESH = pl.DeviceIdType.MESH
ZLO, XS, YS, ZHI = 2, 4, 8, 4
LAT = 512
LATW = 576
SLICE = 12
PARTS = 4
ROWS = SLICE // PARTS
UNIT = 16
score_scale = 192.0 ** (-0.5)
F32 = jnp.float32
BF16 = jnp.bfloat16


def place():
    leaf, head = lax.axis_index("leaf"), lax.axis_index("head")
    return (
        lax.div(leaf, XS * YS), lax.rem(lax.div(leaf, YS), XS), lax.rem(leaf, YS), lax.div(head, 2), lax.rem(head, 2)
    )


def device(zlo, x, y, zhi, core):
    return ((zlo * XS + x) * YS + y, zhi * 2 + core)


def pack(rows, ref, at):
    for block in range(4):
        ref[at + block * ROWS : at + (block + 1) * ROWS, :] = rows[:, block * 128 : (block + 1) * 128]
    ref[at + 12 : at + 13, :] = jnp.concatenate([rows[0:1, LAT:LATW], rows[1:2, LAT:LATW]], axis=1)
    ref[at + 13 : at + 14, 0:64] = rows[2:3, LAT:LATW]


def unpack(value, ref, at):
    for block in range(4):
        ref[at : at + ROWS, block * 128 : (block + 1) * 128] = value[block * ROWS : (block + 1) * ROWS, :]
    ref[at : at + 1, LAT:LATW] = value[12:13, 0:64]
    ref[at + 1 : at + 2, LAT:LATW] = value[12:13, 64:128]
    ref[at + 2 : at + 3, LAT:LATW] = value[13:14, 0:64]


def kernel(
    q_hbm, g_hbm, lat_hbm, ids_hbm, node_hbm, len_hbm,
    att_hbm, node_out, own_out,
    qt, qf, qs, qb, gb, lt, lf, nd, kb, kf, sc, dp, dk, pk, pbt, dst, att,
    ids_all, want, len_ref, pick,
    col, xs, xr, zs, zr, zs2, zr2, xs2, xr2, ys, yr,
    os_, or_, ag,
    sem_local, sem_q, sem_att, sem_ids, sem_y, sem_x, sem_z, sem_z2, sem_x2, sem_y2, sem_o, sem_ag, sem_fin,
):
    zlo, x, y, zhi, core = place()
    other = 1 - core
    half = qb.shape[0] // 2
    heads = qt.shape[0]
    node_keys = kf.shape[0]
    part_keys = node_keys // PARTS
    own_rows = kb.shape[0] - node_keys
    columns = ZLO * YS

    def remote(src, dst_, sems, index, where):
        return pltpu.make_async_remote_copy(
            src_ref=src, dst_ref=dst_, send_sem=sems.at[(0, *index)], recv_sem=sems.at[(1, *index)],
            device_id=where, device_id_type=MESH,
        )

    def column_place(k, sign):
        turn = k // ZLO
        along = YS // 2 + ((turn + 1) // 2) * (1 - 2 * (turn % 2))
        across = ZLO - 1 - k % ZLO
        return lax.rem(zlo + sign * across + ZLO, ZLO), lax.rem(y + sign * along + YS, YS)

    def column_peer(k):
        a, b = column_place(k, 1)
        return device(a, x, b, zhi, core)

    def x_peer(o, c):
        return device(zlo, lax.rem(x + o, XS), y, zhi, lax.rem(core + c, 2))

    def z_peer(o):
        return device(zlo, x, y, lax.rem(zhi + o, ZHI), core)

    x_moves = [(o, c) for o in range(XS) for c in range(2) if o or c]
    node_in = pltpu.make_async_copy(node_hbm, nd, sem_local.at[0])
    node_in.start()

    barrier = pltpu.get_barrier_semaphore()
    for k in range(columns - 1):
        pl.semaphore_signal(barrier, inc=1, device_id=column_peer(k), device_id_type=MESH)

    for o, c in x_moves:
        pl.semaphore_signal(barrier, inc=1, device_id=x_peer(o, c), device_id_type=MESH)
    for o in range(1, ZHI):
        pl.semaphore_signal(barrier, inc=1, device_id=z_peer(o), device_id_type=MESH)

    q_in = pltpu.make_async_copy(q_hbm, qt, sem_local.at[1])
    g_in = pltpu.make_async_copy(g_hbm.at[pl.ds(core * half, half)], gb.at[pl.ds(0, half)], sem_local.at[2])
    lat_in = pltpu.make_async_copy(lat_hbm, lt, sem_local.at[3])
    q_in.start()
    g_in.start()
    lat_in.start()

    ids_in = pltpu.make_async_copy(ids_hbm, ids_all.at[0], sem_local.at[5])
    len_in = pltpu.make_async_copy(len_hbm, len_ref, sem_local.at[6])
    ids_in.start()
    len_in.start()
    mine = zlo * YS + y
    pk[0, :, 0:UNIT, :] = jnp.zeros((PARTS, UNIT, 128), F32)
    node_in.wait()
    slice_rows = nd[...].astype(F32)
    for part in range(PARTS):
        pack(slice_rows[part * ROWS : (part + 1) * ROWS, :], pk.at[0, part], 0)
        col[part][mine] = pk[0, part, 0:UNIT, :].astype(BF16)

    pl.semaphore_wait(barrier, columns - 1 + len(x_moves) + ZHI - 1)

    def ids_copy(o):
        return remote(ids_hbm, ids_all.at[o], sem_ids, (o,), x_peer(o, 0))

    def y_copy(part, k):
        return remote(col[part].at[mine], col[part].at[mine], sem_y, (part, k), column_peer(k))

    for part in range(PARTS):
        for k in range(columns - 1):
            y_copy(part, k).start()

        if part == 0:
            for o in range(1, XS):
                ids_copy(o).start()

    g_swap = remote(g_hbm.at[pl.ds(other * half, half)], gb.at[pl.ds(half, half)], sem_q, (1,), x_peer(0, 1))
    g_swap.start()

    def turn_queries(low, high):
        @pl.loop(low, high)
        def _(h):
            for block in range(5):
                piece = qt[h, block * 128 : min((block + 1) * 128, LATW), :].astype(F32)
                if block == 4:
                    piece = jnp.concatenate([piece, jnp.zeros((64, piece.shape[1]), F32)], axis=0)
                qf[block, pl.ds(h, 2 * own_rows, stride=heads), :] = jnp.transpose(piece)

    q_in.wait()
    turn_queries(0, heads // 2)

    def column_of(node):
        return lax.div(node, XS * YS) * YS + lax.rem(node, YS)

    ids_in.wait()
    len_in.wait()
    for o in range(1, XS):
        ids_copy(o).wait()
    for o in range(XS):
        for leaf in range(2):
            for s in range(3):
                want[o, leaf, s] = column_of(ids_all[o, leaf, s])

    def x_copy(part, o, c):
        return remote(xs.at[part, o, c], xr[part].at[o, c], sem_x, (part, o, c), x_peer(o, c))

    for part in range(PARTS):
        for k in range(columns - 1):
            y_copy(part, k).wait_recv()

        for o in reversed(range(XS)):
            for c in range(2):
                leaf = lax.rem(core + c, 2)
                for s in range(3):
                    piece = col[part][want[(XS - o) % XS, leaf, s]]
                    if o or c:
                        xs[part, o, c, s * UNIT : (s + 1) * UNIT, :] = piece
                    else:
                        xr[part][o, c, s * UNIT : (s + 1) * UNIT, :] = piece
                if o or c:
                    x_copy(part, o, c).start()

    turn_queries(heads // 2, heads)
    for block in range(5):
        to = slice(block * 128, min((block + 1) * 128, LATW))
        for leaf_of, rows_to in ((core, qb), (other, qs)):
            piece = qf[block, pl.ds(pl.multiple_of(leaf_of * half, half), half), :].astype(BF16)
            rows_to[0:half, to] = piece[:, : to.stop - to.start]
    q_swap = remote(qs, qb.at[pl.ds(half, half)], sem_q, (0,), x_peer(0, 1))
    q_swap.start()

    lat_in.wait()
    lf[...] = jnp.transpose(lt[...].astype(F32))
    kb[node_keys:, :] = lf[pl.ds(pl.multiple_of(core * own_rows, own_rows), own_rows), :].astype(BF16)

    def z_copy(part, o):
        return remote(zs.at[part], zr.at[part, o], sem_z, (part, o), z_peer(o))

    for part in range(PARTS):
        for o, c in x_moves:
            x_copy(part, o, c).wait_recv()
        for s in range(3):
            from_x = lax.rem(lax.div(ids_all[0, core, s], YS), XS)
            o = lax.rem(x - from_x + XS, XS)
            for c in range(2):
                at = (c * 3 + s) * UNIT
                zs[part, at : at + UNIT, :] = xr[part][o, c, s * UNIT : (s + 1) * UNIT, :]
        for o in (2, 1, 3):
            if o < ZHI:
                z_copy(part, o).start()

    def unpack_keys(part, o, block):
        for u in range(6):
            unpack(block[u * UNIT : (u + 1) * UNIT, :], kf, part * part_keys + (o * 6 + u) * ROWS)

    def products(at, count):
        keys = kb[at : at + count, :]
        sc[at : at + count, :] = score_scale * lax.dot_general(
            keys, qb[...], (((1,), (1,)), ((), ())), preferred_element_type=F32
        )
        dp[at : at + count, :] = lax.dot_general(
            keys[:, :LAT], gb[...], (((1,), (1,)), ((), ())), preferred_element_type=F32
        )

    length = len_ref[core]
    g_in.wait()
    g_swap.wait()
    q_swap.wait()
    step = min(256, half)

    def live_rows(at):
        first = lax.rem(at, half)
        return (first + lax.broadcasted_iota(jnp.int32, (step, LAT), 0)) // heads < length

    @pl.loop(0, 2 * half // step)
    def _(b):
        at = pl.multiple_of(b * step, step)
        gb[pl.ds(at, step), :] = jnp.where(live_rows(at), gb[pl.ds(at, step), :].astype(F32), 0.0).astype(BF16)

    products(node_keys, own_rows)
    for part in range(PARTS):
        unpack_keys(part, 0, zs[part].astype(F32))
    pk[...] = jnp.zeros(pk.shape, F32)
    for part in range(PARTS):
        for o in (1, 3, 2):
            if o < ZHI:
                z_copy(part, o).wait_recv()
                unpack_keys(part, o, zr[part, o].astype(F32))
        if part % 2:
            at, count = (part - 1) * part_keys, 2 * part_keys
            kb[at : at + count, :] = kf[at : at + count, :].astype(BF16)
            products(at, count)

    @pl.loop(0, 2 * half // step)
    def _(b):
        at = pl.multiple_of(b * step, step)
        first = lax.rem(b * step, half)
        row = (first + lax.broadcasted_iota(jnp.int32, (own_rows, step), 1)) // heads
        seen = lax.broadcasted_iota(jnp.int32, (own_rows, step), 0) <= row
        scores = jnp.concatenate(
            [sc[0:node_keys, pl.ds(at, step)], jnp.where(seen, sc[node_keys:, pl.ds(at, step)], -jnp.inf)], axis=0
        )
        dprobs = dp[:, pl.ds(at, step)]
        top = jnp.max(scores, axis=0, keepdims=True)
        expo = jnp.exp(scores - top)
        probs = expo * (1.0 / jnp.sum(expo, axis=0, keepdims=True))
        probs_b = probs.astype(BF16)
        delta = jnp.sum(probs_b.astype(F32) * dprobs, axis=0, keepdims=True)
        pbt[:, pl.ds(at, step)] = probs_b
        dst[:, pl.ds(at, step)] = (score_scale * probs * (dprobs - delta)).astype(BF16)

    def z2_copy(part, o):
        return remote(zs2.at[part, o], zr2.at[part, o], sem_z2, (part, o), z_peer(o))

    def key_terms(at, count):
        dk[at : at + count, :] = lax.dot_general(
            dst[at : at + count, :], qb[...], (((1,), (0,)), ((), ())), preferred_element_type=F32
        )
        dk[at : at + count, :LAT] += lax.dot_general(
            pbt[at : at + count, :], gb[...], (((1,), (0,)), ((), ())), preferred_element_type=F32
        )

    for part in range(PARTS):
        if part % 2 == 0:
            key_terms(part * part_keys, 2 * part_keys)
        for o in (2, 1, 3, 0):
            if o < ZHI:
                back = (ZHI - o) % ZHI
                for u in range(6):
                    at = part * part_keys + (o * 6 + u) * ROWS
                    pack(dk[at : at + ROWS, :], pk.at[back, part], u * UNIT)
                if back:
                    zs2[part, back] = pk[back, part].astype(BF16)
                    z2_copy(part, back).start()
    key_terms(node_keys, own_rows)

    quarter = own_rows // ZHI

    def o_copy(o):
        return remote(os_.at[o], or_.at[o], sem_o, (o,), z_peer(o))

    for o in range(1, ZHI):
        at = pl.multiple_of(node_keys + lax.rem(zhi + o, ZHI) * quarter, quarter)
        os_[o] = dk[pl.ds(at, quarter), :].astype(BF16)
        o_copy(o).start()

    for group in range(pick.shape[1] // 128):
        lane = lax.broadcasted_iota(jnp.int32, pick.shape[:1] + (128,), 1)
        line = lax.broadcasted_iota(jnp.int32, pick.shape[:1] + (128,), 0)
        goal = jnp.full(lane.shape, -1, jnp.int32)
        for which in range(128 // UNIT):
            term = group * (128 // UNIT) + which
            o, c, s = term // 6, (term // 3) % 2, term % 3
            node = ids_all[o, lax.rem(core + c, 2), s]
            place_ = jnp.where(lax.rem(lax.div(node, YS), XS) == x, column_of(node), -1)
            goal = jnp.where(lane // UNIT == which, place_, goal)
        hit = (line // UNIT == goal) & (line % UNIT == lane % UNIT)
        pick[:, group * 128 : (group + 1) * 128] = jnp.where(hit, 1.0, 0.0).astype(BF16)

    @pl.loop(0, 2 * half // step)
    def _(b):
        at = pl.multiple_of(b * step, step)
        outputs = lax.dot_general(
            pbt[:, pl.ds(at, step)], kb[:, :LAT], (((0,), (0,)), ((), ())), preferred_element_type=F32
        )
        att[pl.ds(at, step), :] = jnp.where(live_rows(at), outputs, 0.0).astype(BF16)

    att_local = pltpu.make_async_copy(att.at[pl.ds(0, half)], att_hbm.at[pl.ds(core * half, half)], sem_local.at[4])
    att_swap = remote(att.at[pl.ds(half, half)], att_hbm.at[pl.ds(core * half, half)], sem_att, (), x_peer(0, 1))
    att_local.start()
    att_swap.start()

    def x2_copy(part, o, c):
        return remote(xs2.at[part, c], xr2.at[part, o, c], sem_x2, (part, o, c), x_peer(o, c))

    def sum_over_z(part):
        total = pk[0, part]
        for o in range(1, ZHI):
            z2_copy(part, o).wait_recv()
            total = total + zr2[part, o].astype(F32)
        total = total.astype(BF16)
        for c in range(2):
            xs2[part, c] = total[c * 3 * UNIT : (c + 1) * 3 * UNIT, :]
        xr2[part, 0, 0] = total[0 : 3 * UNIT, :]
        for o, c in reversed(x_moves):
            x2_copy(part, o, c).start()

    def ag_copy(o):
        return remote(ag.at[0], ag.at[o], sem_ag, (o,), z_peer(o))

    def y2_copy(part, k):
        a, b = column_place(k, 1)
        return remote(ys.at[part, a * YS + b], yr.at[part, k], sem_y2, (part, k), column_peer(k))

    def sum_over_x(part):
        for o, c in x_moves:
            x2_copy(part, o, c).wait_recv()
        terms = xr2[part].reshape(XS * 2 * 3 * UNIT, 128)
        sums = jnp.dot(pick[...], terms, preferred_element_type=F32)
        ys[part] = sums.astype(BF16).reshape(columns, UNIT, 128)
        for k in range(columns - 1):
            y2_copy(part, k).start()

    for part in range(PARTS - 1):
        sum_over_z(part)
    sum_over_x(0)
    sum_over_z(PARTS - 1)
    at = pl.multiple_of(node_keys + zhi * quarter, quarter)
    total = dk[pl.ds(at, quarter), :]
    for o in range(1, ZHI):
        o_copy(o).wait_recv()
        total = total + or_[o].astype(F32)
    ag[0] = total.astype(BF16)
    for o in range(1, ZHI):
        ag_copy(o).start()

    for part in range(1, PARTS):
        sum_over_x(part)

    for o in range(1, ZHI):
        ag_copy(o).wait_recv()
    for o in range(ZHI):
        origin = lax.rem(zhi - o + ZHI, ZHI)
        own_out[core, pl.ds(pl.multiple_of(origin * quarter, quarter), quarter), :] = ag[o]
    fin = remote(own_out.at[core], own_out.at[core], sem_fin, (), x_peer(0, 1))
    fin.start()

    for part in range(PARTS):
        for k in range(columns - 1):
            y_copy(part, k).wait_send()

        for o, c in x_moves:
            x_copy(part, o, c).wait_send()
            x2_copy(part, o, c).wait_send()
        for o in range(1, ZHI):
            z_copy(part, o).wait_send()
            z2_copy(part, o).wait_send()
    for o in range(1, ZHI):
        o_copy(o).wait_send()
        ag_copy(o).wait_send()
    att_local.wait()
    att_swap.wait()

    for part in range(PARTS):
        for k in range(columns - 1):
            y2_copy(part, k).wait_recv()
        total = ys[part, mine].astype(F32)
        for k in range(columns - 1):
            total = total + yr[part, k].astype(F32)
        unpack(total, dk, part * ROWS)
    node_out[...] = dk[0:SLICE, :].astype(BF16)
    fin.wait()
    for part in range(PARTS):
        for k in range(columns - 1):
            y2_copy(part, k).wait_send()


def body(queries, leaf_latent, node_latent, grad_out, leaf_nodes, leaf_lengths):
    rows, heads, width = queries.shape
    total = rows * heads
    own_rows = rows // 2
    node_keys = ZHI * 6 * SLICE
    keys = node_keys + own_rows
    columns = ZLO * YS
    vmem = pl.BlockSpec(memory_space=pltpu.VMEM)
    hbm = pl.BlockSpec(memory_space=pl.ANY)
    dma = pltpu.SemaphoreType.DMA
    flops = 2 * total * keys * (3 * LAT + 2 * LATW)
    att, node_grad, own = pl.pallas_call(
        kernel,
        out_shape=(
            pltpu.VMEM((total, LAT), BF16),
            pltpu.VMEM((SLICE, width), BF16),
            pltpu.VMEM((2, own_rows, width), BF16),
        ),
        in_specs=[hbm, hbm, hbm, hbm, hbm, hbm],
        out_specs=(hbm, vmem, vmem),
        scratch_shapes=[
            pltpu.VMEM((heads, width, rows), BF16),
            pltpu.VMEM((5, total, 128), F32),
            pltpu.VMEM((total // 2, width), BF16),
            pltpu.VMEM((total, width), BF16),
            pltpu.VMEM((total, LAT), BF16),
            pltpu.VMEM((width, rows), BF16),
            pltpu.VMEM((rows, width), F32),
            pltpu.VMEM((SLICE, width), BF16),
            pltpu.VMEM((keys, width), BF16),
            pltpu.VMEM((node_keys, width), F32),
            pltpu.VMEM((keys, total), F32),
            pltpu.VMEM((keys, total), F32),
            pltpu.VMEM((keys, width), F32),
            pltpu.VMEM((ZHI, PARTS, 6 * UNIT, 128), F32),
            pltpu.VMEM((keys, total), BF16),
            pltpu.VMEM((keys, total), BF16),
            pltpu.VMEM((total, LAT), BF16),
            pltpu.SMEM((XS, 2, 3), jnp.int32),
            pltpu.SMEM((XS, 2, 3), jnp.int32),
            pltpu.SMEM((2,), jnp.int32),
            pltpu.VMEM((columns * UNIT, XS * 6 * UNIT), BF16),
            [pltpu.VMEM((columns, UNIT, 128), BF16)] * PARTS,
            pltpu.VMEM((PARTS, XS, 2, 3 * UNIT, 128), BF16),
            [pltpu.VMEM((XS, 2, 3 * UNIT, 128), BF16)] * PARTS,
            pltpu.VMEM((PARTS, 6 * UNIT, 128), BF16),
            pltpu.VMEM((PARTS, ZHI, 6 * UNIT, 128), BF16),
            pltpu.VMEM((PARTS, ZHI, 6 * UNIT, 128), BF16),
            pltpu.VMEM((PARTS, ZHI, 6 * UNIT, 128), BF16),
            pltpu.VMEM((PARTS, 2, 3 * UNIT, 128), BF16),
            pltpu.VMEM((PARTS, XS, 2, 3 * UNIT, 128), BF16),
            pltpu.VMEM((PARTS, columns, UNIT, 128), BF16),
            pltpu.VMEM((PARTS, columns, UNIT, 128), BF16),
            pltpu.VMEM((ZHI, own_rows // ZHI, width), BF16),
            pltpu.VMEM((ZHI, own_rows // ZHI, width), BF16),
            pltpu.VMEM((ZHI, own_rows // ZHI, width), BF16),
            dma((7,)),
            dma((2, 2)),
            dma((2,)),
            dma((2, XS)),
            dma((2, PARTS, columns)),
            dma((2, PARTS, XS, 2)),
            dma((2, PARTS, ZHI)),
            dma((2, PARTS, ZHI)),
            dma((2, PARTS, XS, 2)),
            dma((2, PARTS, columns)),
            dma((2, ZHI)),
            dma((2, ZHI)),
            dma((2,)),
        ],
        compiler_params=pltpu.CompilerParams(
            collective_id=0, has_side_effects=True, vmem_limit_bytes=61 * 2**20
        ),
        cost_estimate=pl.CostEstimate(
            flops=flops, bytes_accessed=2 * total * (width + 2 * LAT), transcendentals=total * keys
        ),
        name="leaves",
    )(
        queries.transpose(1, 2, 0),
        grad_out.reshape(total, LAT),
        leaf_latent.T,
        leaf_nodes,
        node_latent.reshape(SLICE, width),
        leaf_lengths,
    )
    return (
        att.reshape(rows, heads, LAT),
        node_grad.reshape(node_latent.shape),
        own.reshape(rows, width),
    )


def solution(mesh):
    return jax.shard_map(
        body,
        mesh=mesh,
        in_specs=(
            P("leaf", "head", None),
            P("leaf", None),
            P("leaf", "head", None),
            P("leaf", "head", None),
            P("leaf", None),
            P("leaf"),
        ),
        out_specs=(P("leaf", "head", None), P("leaf", "head", None), P("leaf", None)),
        check_vma=False,
    )
```
